512 devices in a mesh: dp: 32 (over z, core), ctx: 16 (over y, x).
Axes of the slice: x: 4, y: 4, z: 16, core: 2. Of those that a mesh axis runs over, the one named last changes fastest.
Arguments:
- tokens: bfloat16 [4096, 7168], P('dp', 'ctx'), may hold values from -6 to 6
- routes: int32 [4096, 2], P('dp'), may hold values from 0 to 31, all different within a row; in each aligned block of 128 rows (0 to 127, 128 to 255, ...) at most 16 rows name the same one
- route_weights: float32 [4096, 2], P('dp'), may hold values from 0.2 to 1.5
- w_gate: bfloat16 [32, 7168, 1024], P('dp', 'ctx'), may hold values from -0.0625 to 0.0625
- w_up: bfloat16 [32, 7168, 1024], P('dp', 'ctx'), may hold values from -0.0625 to 0.0625
- w_down: bfloat16 [32, 1024, 7168], P('dp', None, 'ctx'), may hold values from -0.375 to 0.375
- cotangent: bfloat16 [4096, 7168], P('dp', 'ctx'), may hold values from -6 to 6
Outputs:
- mixed: bfloat16 [4096, 7168], P('dp', 'ctx')
- token_grad: bfloat16 [4096, 7168], P('dp', 'ctx')
The draws below stay inside these ranges and needn't reach their ends.
Inputs may be any that keep to these rules, and one draw needn't show every extreme that they name: Within the tokens of one index of dp no expert is named by more than 16 routes, one expert exactly 16; the routes of a token name distinct experts.
All inputs are finite; a program needn't handle non-finite values.
Results may differ from the reference program's by a relative error of at most 0.03.
Values may be sent and summed in bfloat16 or wider, within the bound.
A program may use at most 64 MiB of HBM per device.

```python
import math
import jax
import jax.numpy as jnp
import numpy as np
from jax import lax

D = 7168
FF = 1024
TOK_DEV = 128
TOPK = 2
EXPERTS = 32
CAP = 16
TOKENS = 4096
N_DP = 32
N_CTX = 16


def shard_levels(stream_key, shape, pieces, smallest, top_value):
    def one(dim, blocks):
        heights = jax.random.uniform(jax.random.fold_in(jax.random.fold_in(stream_key, 6), dim), (blocks,), jnp.float32, smallest / len(pieces), top_value / len(pieces))
        return jnp.repeat(jnp.exp(heights), shape[dim] // blocks).reshape((-1,) + (1,) * (len(shape) - dim - 1))

    factor_of = one(*pieces[0])
    for cut in pieces[1:]:
        factor_of = factor_of * one(*cut)
    return factor_of


def deal_out(stream_key, own, number, rows, amount, top, limit, skew):
    sequence = jax.random.permutation(stream_key, amount)
    crowded, usual = load_shares(amount, rows * top, limit, skew, True), load_shares(amount, rows * top, limit, skew, False)
    places = jnp.arange(amount)

    def named(tallies, rotation):
        used = int((tallies > 0).sum())
        fixed = max(1, used // 4)
        passed = fixed + (places - fixed + rotation * (used - fixed)) % max(1, amount - fixed)
        return jnp.zeros((amount,), jnp.int32).at[sequence[jnp.where(places < fixed, places, passed)]].set(jnp.asarray(tallies, jnp.int32))

    tallies = jnp.where(number % 4 == 0, named(crowded, number // 4), named(usual, number - number // 4 - 1))
    mixed = jax.random.permutation(jax.random.fold_in(own, 3), amount)
    donor, sink = mixed[0:amount // 2 * 2:2], mixed[1:amount // 2 * 2:2]
    margin = jnp.minimum(tallies[donor] - 1, limit - tallies[sink]) // 2
    margin = jnp.where((donor == sequence[0]) | (sink == sequence[0]) | (tallies[sink] == 0), 0, jnp.maximum(margin, 0))
    passed = jax.random.randint(jax.random.fold_in(own, 4), (amount // 2,), 0, 1 << 20) % (margin + 1)
    tallies = tallies.at[donor].add(-passed).at[sink].add(passed)
    labels = jnp.searchsorted(jnp.cumsum(tallies), jnp.arange(rows * top), side="right").astype(jnp.int32)
    listing = labels.reshape(top, rows).T
    listing = listing[jax.random.permutation(jax.random.fold_in(own, 1), rows)]
    rotation = jax.random.randint(jax.random.fold_in(own, 2), (rows, 1), 0, top)
    return jnp.take_along_axis(listing, (jnp.arange(top)[None, :] + rotation) % top, axis=1)


def load_shares(number_of, total, limit, skew, full):
    loads = [(1 << 20) // math.isqrt(grade ** skew) + 1 for grade in range(1, number_of + 1)]
    largest = limit if full else min(limit, max(-(-total // number_of), total * loads[0] // sum(loads)))
    least = 1 if total - largest >= number_of - 1 else 0
    holding, surplus = [largest] + [least] * (number_of - 1), total - largest - least * (number_of - 1)
    while surplus > 0:
        free = [i for i in range(1, number_of) if holding[i] < largest] or [i for i in range(1, number_of) if holding[i] < limit]
        pool, remaining = sum([loads[i] for i in free]), surplus
        for i in free:
            extra = min(limit - holding[i], max(1, remaining * loads[i] // pool), surplus)
            holding[i] = holding[i] + extra
            surplus = surplus - extra
    return np.array(holding)


def gaussian(own_key, extent, deviation, limit, split=(), kind=jnp.bfloat16):
    values = deviation * jax.random.normal(own_key, extent, jnp.float32)
    if split:
        values = values * shard_levels(own_key, extent, split, -0.22, 0.18)
    return jnp.clip(values, -limit, limit).astype(kind)


def setup_inputs(seed: int = 0) -> dict:
    arg_keys = jax.random.split(jax.random.key(seed), 8)
    tokens = gaussian(arg_keys[0], (TOKENS, D), 1.0, 6.0, ((0, 32), (1, 16)))
    routes_keys = jax.random.split(jax.random.fold_in(arg_keys[1], 1), TOKENS // TOK_DEV)
    routes_turns = jax.random.permutation(jax.random.fold_in(arg_keys[1], 3), TOKENS // TOK_DEV)
    routes = jax.vmap(lambda own, number: deal_out(jax.random.fold_in(arg_keys[1], 2), own, number, TOK_DEV, EXPERTS, TOPK, CAP, 2))(routes_keys, routes_turns).reshape((TOKENS, TOPK))
    route_weights = jnp.clip(0.2 + 1.3 * jax.random.uniform(arg_keys[2], (TOKENS, TOPK), jnp.float32) ** shard_levels(arg_keys[2], (TOKENS, TOPK), ((0, 32),), -0.2, 0.2), 0.2, 1.5)
    w_gate = gaussian(arg_keys[3], (EXPERTS, D, FF), D ** -0.5, 0.0625, ((0, 32), (1, 16)))
    w_up = gaussian(arg_keys[4], (EXPERTS, D, FF), D ** -0.5, 0.0625, ((0, 32), (1, 16)))
    w_down = gaussian(arg_keys[5], (EXPERTS, FF, D), (FF // 4) ** -0.5, 0.375, ((0, 32), (2, 16)))
    cotangent = gaussian(arg_keys[6], (TOKENS, D), 1.0, 6.0, ((0, 32), (1, 16)))
    return dict(tokens=tokens, routes=routes, route_weights=route_weights, w_gate=w_gate, w_up=w_up, w_down=w_down, cotangent=cotangent)


def route_columns(routes):
    flat = routes.reshape(N_DP, TOK_DEV * TOPK)
    onehot = (flat[:, :, None] == jnp.arange(EXPERTS, dtype=jnp.int32)[None, None, :]).astype(jnp.int32)
    before = jnp.cumsum(onehot, axis=1) - onehot
    slot = jnp.sum(before * onehot, axis=2)
    block = jnp.arange(N_DP, dtype=jnp.int32)[:, None]
    return (block * CAP + slot).reshape(-1), routes.reshape(-1)


def block_sum(left, right):
    left_blocks = left.astype(jnp.float32).reshape(left.shape[0], N_CTX, -1)
    right_blocks = right.astype(jnp.float32).reshape(N_CTX, -1, right.shape[1])
    parts = jnp.einsum("rcd,cdf->crf", left_blocks, right_blocks, precision=lax.Precision.HIGHEST)
    rounded = lax.optimization_barrier(parts.astype(jnp.bfloat16))
    return jnp.sum(rounded.astype(jnp.float32), axis=0)


def reference(tokens, routes, route_weights, w_gate, w_up, w_down, cotangent):
    column, expert_of = route_columns(routes)
    gflat = route_weights.reshape(-1)
    row_ids = jnp.arange(N_DP * CAP, dtype=jnp.int32)
    tok_f = tokens.astype(jnp.float32)
    cot_f = cotangent.astype(jnp.float32)

    def one_expert(carry, item):
        mixed, grad = carry
        wg, wu, wd, index = item
        hit = ((column[None, :] == row_ids[:, None]) & (expert_of[None, :] == index)).astype(jnp.float32)
        pick = hit.reshape(N_DP * CAP, TOKENS, TOPK).sum(-1)
        weighted = (hit * gflat[None, :]).reshape(N_DP * CAP, TOKENS, TOPK).sum(-1)
        rows = jnp.dot(pick, tok_f, precision=lax.Precision.HIGHEST).astype(jnp.bfloat16)
        gate = block_sum(rows, wg)
        up = block_sum(rows, wu)
        sig = jax.nn.sigmoid(gate)
        hidden = (gate * sig * up).astype(jnp.bfloat16)
        expert_out = jnp.dot(hidden, wd, preferred_element_type=jnp.float32).astype(jnp.bfloat16)
        mixed = mixed + jnp.dot(weighted.T, expert_out.astype(jnp.float32), precision=lax.Precision.HIGHEST)
        out_grad = jnp.dot(weighted, cot_f, precision=lax.Precision.HIGHEST).astype(jnp.bfloat16)
        hidden_grad = block_sum(out_grad, wd.T)
        gate_grad = (hidden_grad * up * sig * (1.0 + gate * (1.0 - sig))).astype(jnp.bfloat16)
        up_grad = (hidden_grad * gate * sig).astype(jnp.bfloat16)
        row_grad = (jnp.dot(gate_grad, wg.T, preferred_element_type=jnp.float32)
                    + jnp.dot(up_grad, wu.T, preferred_element_type=jnp.float32)).astype(jnp.bfloat16)
        grad = grad + jnp.dot(pick.T, row_grad.astype(jnp.float32), precision=lax.Precision.HIGHEST)
        return (mixed, grad), None

    start = (jnp.zeros((TOKENS, D), jnp.float32), jnp.zeros((TOKENS, D), jnp.float32))
    items = (w_gate, w_up, w_down, jnp.arange(EXPERTS, dtype=jnp.int32))
    (mixed, grad), _ = lax.scan(one_expert, start, items)
    return mixed.astype(jnp.bfloat16), grad.astype(jnp.bfloat16)
```

```python
import functools

import jax
import jax.numpy as jnp
from jax import lax
from jax.experimental import pallas as pl
from jax.experimental.pallas import tpu as pltpu
from jax.sharding import PartitionSpec as P

MESH = pl.DeviceIdType.MESH
BF = jnp.bfloat16
F32 = jnp.float32

NZ = 16
NDP = 32
CAP = 16
NB = 8
COLS = 448
PAIR = 2 * COLS
FF = 1024
PAD = 64


def chip_at(z, k):
    off = ((k + 1) // 2) * (2 * (k % 2) - 1)
    return (z + NZ + off) % NZ


def mirror(k):
    odd = k % 2
    inner = jnp.where((k == 0) | (k == NZ - 1), 0, 2 * odd - 1)
    return k + inner


def nt(a, b):
    return lax.dot_general(a, b, (((1,), (1,)), ((), ())), preferred_element_type=F32)


def nn(a, b):
    return jnp.dot(a, b, preferred_element_type=F32)


def kernel(
    tok_hbm, routes_ref, rw_ref, wg_hbm, wu_hbm, wd_hbm, cot_hbm,
    mixed_ref, grad_ref,
    tok, cot, wd_in, wg, wu, wd_l, wd_r,
    xs, xr, p1s, p1r, p2s, p2r, h1, h2, rs, rr, pt0, pt1,
    in_sem, send_sem, x_sem, p1_sem, p2_sem, h1_sem, h2_sem, r_sem,
):
    dp = lax.axis_index("dp")
    ctx = lax.axis_index("ctx")
    z, y, x = dp // 2, ctx // 4, ctx % 4

    barrier = pltpu.get_barrier_semaphore()

    def greet_dp(k, carry):
        pl.semaphore_signal(barrier, inc=1, device_id={"dp": (dp + k) % NDP}, device_id_type=MESH)
        return carry

    def greet_ctx(k, carry):
        pl.semaphore_signal(barrier, inc=1, device_id={"ctx": (ctx + k) % 16}, device_id_type=MESH)
        return carry

    loads = [
        pltpu.make_async_copy(tok_hbm, tok, in_sem.at[0]),
        pltpu.make_async_copy(cot_hbm, cot, in_sem.at[1]),
        pltpu.make_async_copy(wg_hbm, wg.at[pl.ds(PAD, COLS)], in_sem.at[2]),
        pltpu.make_async_copy(wu_hbm, wu.at[pl.ds(PAD, COLS)], in_sem.at[3]),
        pltpu.make_async_copy(wd_hbm, wd_in, in_sem.at[4]),
    ]
    lax.fori_loop(1, NDP, greet_dp, 0)
    lax.fori_loop(1, 16, greet_ctx, 0)
    for load in loads:
        load.start()

    r0, r1 = routes_ref[:, 0:1], routes_ref[:, 1:2]
    w0, w1 = rw_ref[:, 0:1], rw_ref[:, 1:2]
    rows = routes_ref.shape[0]
    experts = lax.broadcasted_iota(jnp.int32, (rows, 128), 1)
    oh0 = (r0 == experts).astype(F32)
    oh1 = (r1 == experts).astype(F32)
    earlier = (
        lax.broadcasted_iota(jnp.int32, (rows, rows), 1)
        < lax.broadcasted_iota(jnp.int32, (rows, rows), 0)
    ).astype(F32)
    before = nn(earlier.astype(BF), (oh0 + oh1).astype(BF))
    s0 = jnp.sum(before * oh0, axis=1, keepdims=True).astype(jnp.int32)
    s1 = jnp.sum(before * oh1, axis=1, keepdims=True).astype(jnp.int32)
    places = lax.broadcasted_iota(jnp.int32, (rows, NDP * CAP), 1)
    hit0 = (r0 * CAP + s0 == places).astype(F32)
    hit1 = (r1 * CAP + s1 == places).astype(F32)
    pt0[...] = hit0
    pt1[...] = hit1
    loads[0].wait()
    loads[1].wait()
    cot_f = cot[...].astype(F32)
    both = jnp.concatenate(
        [
            jnp.concatenate([tok[...].astype(F32), cot_f * w0], axis=1),
            jnp.concatenate([tok[...].astype(F32), cot_f * w1], axis=1),
        ],
        axis=0,
    ).astype(BF)
    pick = jnp.concatenate([hit0, hit1], axis=0).T.astype(BF)
    xs[...] = nn(pick, both).astype(BF).reshape(NDP, CAP, PAIR)

    pl.semaphore_wait(barrier, NDP - 1 + 15)

    def dispatch(k, carry):
        chip = chip_at(z, k)
        place = mirror(k)
        for core in range(2):
            dst = chip * 2 + core

            @pl.when(dst != dp)
            def _():
                pltpu.make_async_remote_copy(
                    src_ref=xs.at[dst], dst_ref=xr.at[dp], send_sem=send_sem.at[0],
                    recv_sem=x_sem.at[place], device_id={"dp": dst}, device_id_type=MESH,
                ).start()

        return carry

    lax.fori_loop(0, NZ, dispatch, 0)
    xr[dp] = xs[dp]

    zero = jnp.zeros((PAD, FF), BF)
    for w in (wg, wu):
        w[0:PAD] = zero
        w[PAD + COLS :] = zero
    loads[4].wait()

    def widen(i, carry):
        part = pl.ds(pl.multiple_of(i * 128, 128), 128)
        block = wd_in[part].astype(F32)
        blank = jnp.zeros((128, PAD), F32)
        wd_l[part] = jnp.concatenate([blank, block], axis=1).astype(BF)
        wd_r[part] = jnp.concatenate([block, blank], axis=1).astype(BF)
        return carry

    lax.fori_loop(0, FF // 128, widen, 0)
    loads[2].wait()
    loads[3].wait()

    def peer(along_x, d):
        if along_x:
            return y * 4 + (x + d) % 4
        return ((y + d) % 4) * 4 + x

    def send(src, dst, kind, recv, along_x, d):
        pltpu.make_async_remote_copy(
            src_ref=src, dst_ref=dst, send_sem=send_sem.at[kind], recv_sem=recv,
            device_id={"ctx": peer(along_x, d)}, device_id_type=MESH,
        ).start()

    def await_bytes(ref, sem):
        pltpu.make_async_copy(ref, ref, sem).wait()

    def first(g):
        return x if g == 0 else y

    def second(g):
        return y if g == 0 else x

    def products(b):
        @pl.when(b == 0)
        def _():
            await_bytes(xr.at[pl.ds(0, 1)], x_sem.at[0])

        @pl.when(b > 0)
        def _():
            await_bytes(xr.at[pl.ds(0, 2)], x_sem.at[2 * b])

        await_bytes(xr.at[pl.ds(0, 2)], x_sem.at[2 * b + 1])
        block = jnp.concatenate(
            [
                xr[pl.ds(2 * chip_at(z, 2 * b + g), 2)].reshape(2 * CAP, PAIR)
                for g in range(2)
            ],
            axis=0,
        )
        left, right = block[:, 0:512], block[:, 384:896]
        parts = (
            nn(left, wg[PAD : PAD + 512]),
            nn(left, wu[PAD : PAD + 512]),
            nt(right, wd_l[...]),
        )
        for g in range(2):
            for p in range(4):
                for a in range(3):
                    p1s[b, g, p, :, a * 256 : a * 256 + 256] = parts[a][
                        g * 32 : g * 32 + 32, p * 256 : p * 256 + 256
                    ].astype(BF)
        for d in range(1, 4):
            for g in range(2):
                send(
                    p1s.at[b, g, (first(g) + d) % 4], p1r.at[b, g, d - 1], 1, p1_sem.at[b], g == 0, d
                )

    def add_first(b):
        await_bytes(p1r.at[b], p1_sem.at[b])
        for g in range(2):
            total = p1s[b, g, first(g)].astype(F32)
            for d in range(3):
                total = total + p1r[b, g, d].astype(F32)
            for q in range(4):
                for a in range(3):
                    lane = a * 256 + 128 * (q % 2)
                    p2s[b, g, q, :, a * 128 : a * 128 + 128] = total[
                        16 * (q // 2) : 16 * (q // 2) + 16, lane : lane + 128
                    ].astype(BF)
        for d in range(1, 4):
            for g in range(2):
                send(
                    p2s.at[b, g, (second(g) + d) % 4], p2r.at[b, g, d - 1], 2, p2_sem.at[b], g == 1, d
                )

    def add_second(b):
        await_bytes(p2r.at[b], p2_sem.at[b])
        for g in range(2):
            total = p2s[b, g, second(g)].astype(F32)
            for d in range(3):
                total = total + p2r[b, g, d].astype(F32)
            gate, up, hidden_grad = total[:, 0:128], total[:, 128:256], total[:, 256:384]
            sig = jax.nn.sigmoid(gate)
            h1[b, g, second(g), :, 0:128] = (gate * sig * up).astype(BF)
            h1[b, g, second(g), :, 128:256] = (
                hidden_grad * up * sig * (1.0 + gate * (1.0 - sig))
            ).astype(BF)
            h1[b, g, second(g), :, 256:384] = (hidden_grad * gate * sig).astype(BF)
        for d in range(1, 4):
            for g in range(2):
                mine = h1.at[b, g, second(g)]
                send(mine, mine, 3, h1_sem.at[b], g == 1, d)

    def spread(b):
        await_bytes(p2r.at[b], h1_sem.at[b])
        for d in range(1, 4):
            for g in range(2):
                send(h1.at[b, g], h2.at[b, g, first(g)], 4, h2_sem.at[b], g == 0, d)
        for g in range(2):
            h2[b, g, first(g)] = h1[b, g]

    def give_back(b):
        await_bytes(p1r.at[b], h2_sem.at[b])

        def whole(a):
            return jnp.concatenate(
                [
                    jnp.concatenate(
                        [
                            h2[b, g, p, 2 * half + q, :, a * 128 : a * 128 + 128]
                            for p in range(4)
                            for q in range(2)
                        ],
                        axis=1,
                    )
                    for g in range(2)
                    for half in range(2)
                ],
                axis=0,
            )

        out = nn(whole(0), wd_r[...])
        row_grad = nt(whole(1), wg[0:512]) + nt(whole(2), wu[0:512])
        pair = jnp.concatenate(
            [out[:, 0:384], out[:, 384:512] + row_grad[:, 0:128], row_grad[:, 128:512]], axis=1
        ).astype(BF)
        for g in range(2):
            for core in range(2):
                dst = chip_at(z, 2 * b + g) * 2 + core
                at = (2 * g + core) * CAP
                rs[dst] = pair[at : at + CAP]

                @pl.when(dst != dp)
                def _():
                    pltpu.make_async_remote_copy(
                        src_ref=rs.at[dst], dst_ref=rr.at[dp], send_sem=send_sem.at[5],
                        recv_sem=r_sem.at[0], device_id={"dp": dst}, device_id_type=MESH,
                    ).start()

    stages = (products, add_first, add_second, spread, give_back)

    def step(t, carry):
        for s in reversed(range(len(stages))):
            b = t - s

            @pl.when((b >= 0) & (b < NB))
            def _():
                stages[s](b)

        return carry

    lax.fori_loop(0, NB + len(stages) - 1, step, 0)
    rr[dp] = rs[dp]

    hit0, hit1 = pt0[...], pt1[...]
    weighted = hit0 * rw_ref[:, 0:1] + hit1 * rw_ref[:, 1:2]
    high = weighted.astype(BF)
    low = (weighted - high.astype(F32)).astype(BF)
    plain = (hit0 + hit1).astype(BF)
    await_bytes(rr.at[pl.ds(0, NDP - 1)], r_sem.at[0])
    back = rr[...].reshape(NDP * CAP, PAIR)
    mixed_ref[...] = (nn(high, back[:, 0:512]) + nn(low, back[:, 0:512]))[:, 0:COLS].astype(BF)
    grad_ref[...] = nn(plain, back[:, 384:896])[:, PAD:].astype(BF)

    await_bytes(xs.at[pl.ds(0, NDP - 1)], send_sem.at[0])
    await_bytes(p1r, send_sem.at[1])
    await_bytes(p2r, send_sem.at[2])
    await_bytes(p2r, send_sem.at[3])
    await_bytes(p1r, send_sem.at[4])
    await_bytes(xs.at[pl.ds(0, NDP - 1)], send_sem.at[5])


def shards(tokens, routes, route_weights, w_gate, w_up, w_down, cotangent):
    rows, cols = tokens.shape
    hbm = pl.BlockSpec(memory_space=pl.ANY)
    vmem = pl.BlockSpec(memory_space=pltpu.VMEM)
    dma = pltpu.SemaphoreType.DMA
    out = jax.ShapeDtypeStruct((rows, cols), BF)
    return pl.pallas_call(
        kernel,
        out_shape=(out, out),
        in_specs=[hbm, vmem, vmem, hbm, hbm, hbm, hbm],
        out_specs=(vmem, vmem),
        scratch_shapes=[
            pltpu.VMEM((rows, cols), BF),
            pltpu.VMEM((rows, cols), BF),
            pltpu.VMEM((FF, COLS), BF),
            pltpu.VMEM((PAD + COLS + PAD, FF), BF),
            pltpu.VMEM((PAD + COLS + PAD, FF), BF),
            pltpu.VMEM((FF, 512), BF),
            pltpu.VMEM((FF, 512), BF),
            pltpu.VMEM((NDP, CAP, PAIR), BF),
            pltpu.VMEM((NDP, CAP, PAIR), BF),
            pltpu.VMEM((NB, 2, 4, 32, 768), BF),
            pltpu.VMEM((NB, 2, 3, 32, 768), BF),
            pltpu.VMEM((NB, 2, 4, 16, 384), BF),
            pltpu.VMEM((NB, 2, 3, 16, 384), BF),
            pltpu.VMEM((NB, 2, 4, 16, 384), BF),
            pltpu.VMEM((NB, 2, 4, 4, 16, 384), BF),
            pltpu.VMEM((NDP, CAP, PAIR), BF),
            pltpu.VMEM((NDP, CAP, PAIR), BF),
            pltpu.VMEM((rows, NDP * CAP), F32),
            pltpu.VMEM((rows, NDP * CAP), F32),
            dma((5,)),
            dma((6,)),
            dma((NZ,)),
            dma((NB,)),
            dma((NB,)),
            dma((NB,)),
            dma((NB,)),
            dma((1,)),
        ],
        compiler_params=pltpu.CompilerParams(
            collective_id=0, has_side_effects=True, vmem_limit_bytes=48 << 20
        ),
        cost_estimate=pl.CostEstimate(
            flops=6 * 2 * 512 * COLS * FF, bytes_accessed=4 << 20, transcendentals=1 << 16
        ),
    )(tokens, routes, route_weights, w_gate[0], w_up[0], w_down[0], cotangent)


def solution(mesh):
    in_specs = (
        P("dp", "ctx"),
        P("dp", None),
        P("dp", None),
        P("dp", "ctx", None),
        P("dp", "ctx", None),
        P("dp", None, "ctx"),
        P("dp", "ctx"),
    )
    out_specs = (P("dp", "ctx"), P("dp", "ctx"))
    return jax.shard_map(shards, mesh=mesh, in_specs=in_specs, out_specs=out_specs, check_vma=False)
```

```python
import functools

import jax
import jax.numpy as jnp
from jax import lax
from jax.experimental import pallas as pl
from jax.experimental.pallas import tpu as pltpu
from jax.sharding import PartitionSpec as P

LOGICAL = pl.DeviceIdType.LOGICAL
BF = jnp.bfloat16
F32 = jnp.float32

NZ = 16
NDP = 32
CAP = 16
NB = 8
COLS = 448
PAIR = 2 * COLS
FF = 1024
PAD = 64


FAR = (2, 7, 6, 5, 4, 3, 1, 0)
PLAN = (
    (0, 0), (1, 0), (2, 0), (0, 1), (3, 0), (1, 1), (0, 2), (4, 0),
    (2, 1), (1, 2), (3, 1), (0, 3), (2, 2), (4, 1), (1, 3), (3, 2),
    (0, 4), (2, 3), (4, 2), (0, 5), (3, 3), (1, 4), (0, 6), (0, 7),
    (2, 4), (1, 5), (4, 3), (3, 4), (1, 6), (1, 7), (2, 5), (2, 6),
    (2, 7), (4, 4), (3, 5), (3, 6), (3, 7), (4, 5), (4, 6), (4, 7),
)


def entry(values, i):
    found = values[-1]
    for n, value in enumerate(values[:-1]):
        found = jnp.where(i == n, value, found)
    return found


def offset_at(b, g):
    far = entry(FAR, b)
    return far + 1 if g == 0 else -far


def wrap(i, n):
    return jnp.where(i < 0, i + n, jnp.where(i >= n, i - n, i))


def nt(a, b):
    return lax.dot_general(a, b, (((1,), (1,)), ((), ())), preferred_element_type=F32)


def nn(a, b):
    return jnp.dot(a, b, preferred_element_type=F32)


def kernel(
    tok_hbm, routes_hbm, rw_hbm, wg_hbm, wu_hbm, wd_hbm, cot_hbm,
    mixed_ref, grad_ref,
    tok, cot, routes, weights, wg, wu, wd,
    xs, xr, p1s, p1r, p2s, p2r, h1, h2, rs, rr, weigh_hi, weigh_lo, plain,
    in_sem, send_sem, x_sem, p1_sem, p2_sem, h1_sem, h2_sem, r_sem,
):
    dp = lax.axis_index("dp")
    ctx = lax.axis_index("ctx")
    z, y, x = dp // 2, ctx // 4, ctx % 4

    def await_bytes(ref, sem):
        pltpu.make_async_copy(ref, ref, sem).wait()

    barrier = pltpu.get_barrier_semaphore()

    def greet_dp(k, carry):
        pl.semaphore_signal(barrier, inc=1, device_id=wrap(dp + k, NDP) * 16 + ctx, device_id_type=LOGICAL)
        return carry

    def greet_ctx(k, carry):
        pl.semaphore_signal(barrier, inc=1, device_id=dp * 16 + wrap(ctx + k, 16), device_id_type=LOGICAL)
        return carry

    loads = [
        pltpu.make_async_copy(routes_hbm, routes, in_sem.at[5]),
        pltpu.make_async_copy(rw_hbm, weights, in_sem.at[6]),
        pltpu.make_async_copy(tok_hbm, tok, in_sem.at[0]),
        pltpu.make_async_copy(cot_hbm, cot, in_sem.at[1]),
        pltpu.make_async_copy(wg_hbm, wg.at[pl.ds(PAD, COLS)], in_sem.at[2]),
        pltpu.make_async_copy(wu_hbm, wu.at[pl.ds(PAD, COLS)], in_sem.at[3]),
        pltpu.make_async_copy(wd_hbm, wd.at[pl.ds(PAD, COLS)], in_sem.at[4]),
    ]
    for load in loads:
        load.start()
    lax.fori_loop(1, NDP, greet_dp, 0)
    lax.fori_loop(1, 16, greet_ctx, 0)

    loads[0].wait()
    loads[1].wait()
    r0, r1 = routes[0:1].astype(F32), routes[1:2].astype(F32)
    w0, w1 = weights[0:1], weights[1:2]
    rows = routes.shape[1]
    experts = lax.broadcasted_iota(jnp.int32, (NDP, rows), 0).astype(F32)
    oh0 = (r0 == experts).astype(F32)
    oh1 = (r1 == experts).astype(F32)
    earlier = (
        lax.broadcasted_iota(jnp.int32, (rows, rows), 0)
        < lax.broadcasted_iota(jnp.int32, (rows, rows), 1)
    ).astype(F32)
    before = nn((oh0 + oh1).astype(BF), earlier.astype(BF))
    s0 = jnp.sum(before * oh0, axis=0, keepdims=True)
    s1 = jnp.sum(before * oh1, axis=0, keepdims=True)
    places = lax.broadcasted_iota(jnp.int32, (NDP * CAP, rows), 0).astype(F32)
    hit0 = (r0 * CAP + s0 == places).astype(F32)
    hit1 = (r1 * CAP + s1 == places).astype(F32)
    loads[2].wait()
    loads[3].wait()
    tok_f, cot_f = tok[...].astype(F32), cot[...].astype(F32)
    both = jnp.concatenate(
        [
            jnp.concatenate([tok_f, tok_f], axis=1),
            jnp.concatenate([cot_f * w0, cot_f * w1], axis=1),
        ],
        axis=0,
    ).astype(BF)
    pick = jnp.concatenate([hit0, hit1], axis=1).astype(BF)
    xs[...] = nt(pick, both).astype(BF).reshape(NDP, CAP, PAIR)

    pl.semaphore_wait(barrier, NDP - 1 + 15)

    def z_send(src, dst, dst_dp, kind, recv):
        pltpu.make_async_remote_copy(
            src_ref=src, dst_ref=dst, send_sem=send_sem.at[kind], recv_sem=recv,
            device_id=dst_dp * 16 + ctx, device_id_type=LOGICAL,
        ).start()

    def dispatch(b, carry):
        for g in range(2):
            off = offset_at(b, g)
            for c in range(2):
                dst = (wrap(z - off, NZ)) * 2 + c

                @pl.when(dst != dp)
                def _():
                    z_send(xs.at[dst], xr.at[dp], dst, 0, x_sem.at[2 * b + g])

        return carry

    lax.fori_loop(0, NB, dispatch, 0)
    xr[dp] = xs[dp]

    zero = jnp.zeros((PAD, FF), BF)
    for w in (wg, wu, wd):
        w[0:PAD] = zero
        w[PAD + COLS :] = zero
    weighted = (hit0 * w0 + hit1 * w1).T
    high = weighted.astype(BF)
    weigh_hi[...] = high
    weigh_lo[...] = (weighted - high.astype(F32)).astype(BF)
    plain[...] = (hit0 + hit1).T.astype(BF)
    for load in loads[4:]:
        load.wait()

    x_at = [wrap(x + d, 4) for d in range(4)]
    y_at = [wrap(y + d, 4) for d in range(4)]
    peers = {
        True: [dp * 16 + y * 4 + x_at[d] for d in range(1, 4)],
        False: [dp * 16 + y_at[d] * 4 + x for d in range(1, 4)],
    }

    def send(src, dst, kind, recv, along_x, d):
        pltpu.make_async_remote_copy(
            src_ref=src, dst_ref=dst, send_sem=send_sem.at[kind], recv_sem=recv,
            device_id=peers[along_x][d - 1], device_id_type=LOGICAL,
        ).start()

    def first(g, d=0):
        return x_at[d] if g == 0 else y_at[d]

    def second(g, d=0):
        return y_at[d] if g == 0 else x_at[d]

    def products(b):
        await_bytes(xr.at[pl.ds(0, 2)], x_sem.at[2 * b])

        here = offset_at(b, 1) == 0

        @pl.when(here)
        def _():
            await_bytes(xr.at[pl.ds(0, 1)], x_sem.at[2 * b + 1])

        @pl.when(jnp.logical_not(here))
        def _():
            await_bytes(xr.at[pl.ds(0, 2)], x_sem.at[2 * b + 1])

        block = jnp.concatenate(
            [
                xr[pl.ds(2 * (wrap(z + offset_at(b, g), NZ)), 2)].reshape(2 * CAP, PAIR)
                for g in range(2)
            ],
            axis=0,
        )
        left, right = block[:, 0:512], block[:, 384:896]
        parts = (
            nn(left, wg[PAD : PAD + 512]),
            nn(left, wu[PAD : PAD + 512]),
            nn(right, wd[0:512]),
        )
        for g in range(2):
            for p in range(4):
                for a in range(3):
                    p1s[b, g, p, :, a * 256 : a * 256 + 256] = parts[a][
                        g * 32 : g * 32 + 32, p * 256 : p * 256 + 256
                    ].astype(BF)
        for d in range(1, 4):
            for g in range(2):
                send(
                    p1s.at[b, g, first(g, d)], p1r.at[b, g, d - 1], 1, p1_sem.at[b], g == 0, d
                )

    def add_first(b):
        await_bytes(p1r.at[b], p1_sem.at[b])
        for g in range(2):
            total = p1s[b, g, first(g)].astype(F32)
            for d in range(3):
                total = total + p1r[b, g, d].astype(F32)
            for q in range(4):
                for a in range(3):
                    lane = a * 256 + 128 * (q % 2)
                    p2s[b, g, q, :, a * 128 : a * 128 + 128] = total[
                        16 * (q // 2) : 16 * (q // 2) + 16, lane : lane + 128
                    ].astype(BF)
        for d in range(1, 4):
            for g in range(2):
                send(
                    p2s.at[b, g, second(g, d)], p2r.at[b, g, d - 1], 2, p2_sem.at[b], g == 1, d
                )

    def add_second(b):
        await_bytes(p2r.at[b], p2_sem.at[b])
        for g in range(2):
            total = p2s[b, g, second(g)].astype(F32)
            for d in range(3):
                total = total + p2r[b, g, d].astype(F32)
            gate, up, hidden_grad = total[:, 0:128], total[:, 128:256], total[:, 256:384]
            sig = jax.nn.sigmoid(gate)
            h1[b, g, second(g), :, 0:128] = (gate * sig * up).astype(BF)
            h1[b, g, second(g), :, 128:256] = (
                hidden_grad * up * sig * (1.0 + gate * (1.0 - sig))
            ).astype(BF)
            h1[b, g, second(g), :, 256:384] = (hidden_grad * gate * sig).astype(BF)
        for d in range(1, 4):
            for g in range(2):
                mine = h1.at[b, g, second(g)]
                send(mine, mine, 3, h1_sem.at[b], g == 1, d)

    def spread(b):
        await_bytes(p2r.at[b], h1_sem.at[b])
        for d in range(1, 4):
            for g in range(2):
                send(h1.at[b, g], h2.at[b, g, first(g)], 4, h2_sem.at[b], g == 0, d)
        for g in range(2):
            h2[b, g, first(g)] = h1[b, g]

    def give_back(b):
        await_bytes(p1r.at[b], h2_sem.at[b])

        def whole(a):
            return jnp.concatenate(
                [
                    jnp.concatenate(
                        [
                            h2[b, g, p, 2 * half + q, :, a * 128 : a * 128 + 128]
                            for p in range(4)
                            for q in range(2)
                        ],
                        axis=1,
                    )
                    for g in range(2)
                    for half in range(2)
                ],
                axis=0,
            )

        out = nt(whole(0), wd[PAD : PAD + 512])
        row_grad = nt(whole(1), wg[0:512]) + nt(whole(2), wu[0:512])
        pair = jnp.concatenate(
            [out[:, 0:384], out[:, 384:512] + row_grad[:, 0:128], row_grad[:, 128:512]], axis=1
        ).astype(BF)
        for g in range(2):
            off = offset_at(b, g)
            for c in range(2):
                dst = (wrap(z + off, NZ)) * 2 + c
                at = (2 * g + c) * CAP
                rs[dst] = pair[at : at + CAP]

                @pl.when(dst != dp)
                def _():
                    z_send(rs.at[dst], rr.at[dp], dst, 5, r_sem.at[0])

    stages = (products, add_first, add_second, spread, give_back)

    def step(n, carry):
        code = entry(tuple(s * NB + b for s, b in PLAN), n)
        for s, work in enumerate(stages):

            @pl.when((code >= s * NB) & (code < s * NB + NB))
            def _():
                work(code - s * NB)

        return carry

    lax.fori_loop(0, len(PLAN), step, 0)
    rr[dp] = rs[dp]

    await_bytes(rr.at[pl.ds(0, NDP - 1)], r_sem.at[0])
    back = rr[...].reshape(NDP * CAP, PAIR)
    mixed = nn(weigh_hi[...], back[:, 0:512]) + nn(weigh_lo[...], back[:, 0:512])
    grad = nn(plain[...], back[:, 384:896])
    mixed_ref[...] = mixed.T[0:COLS].astype(BF)
    grad_ref[...] = grad.T[PAD:].astype(BF)

    await_bytes(xs.at[pl.ds(0, NDP - 1)], send_sem.at[0])
    await_bytes(p1r, send_sem.at[1])
    await_bytes(p2r, send_sem.at[2])
    await_bytes(p2r, send_sem.at[3])
    await_bytes(p1r, send_sem.at[4])
    await_bytes(xs.at[pl.ds(0, NDP - 1)], send_sem.at[5])


def shards(tokens, routes, route_weights, w_gate, w_up, w_down, cotangent):
    rows, cols = tokens.shape
    hbm = pl.BlockSpec(memory_space=pltpu.HBM)
    vmem = pl.BlockSpec(memory_space=pltpu.VMEM)
    dma = pltpu.SemaphoreType.DMA
    out = jax.ShapeDtypeStruct((cols, rows), BF)
    mixed, grad = pl.pallas_call(
        kernel,
        out_shape=(out, out),
        in_specs=[hbm, hbm, hbm, hbm, hbm, hbm, hbm],
        out_specs=(vmem, vmem),
        scratch_shapes=[
            pltpu.VMEM((cols, rows), BF),
            pltpu.VMEM((cols, rows), BF),
            pltpu.VMEM(routes.shape[::-1], jnp.int32),
            pltpu.VMEM(routes.shape[::-1], F32),
            pltpu.VMEM((PAD + COLS + PAD, FF), BF),
            pltpu.VMEM((PAD + COLS + PAD, FF), BF),
            pltpu.VMEM((PAD + COLS + PAD, FF), BF),
            pltpu.VMEM((NDP, CAP, PAIR), BF),
            pltpu.VMEM((NDP, CAP, PAIR), BF),
            pltpu.VMEM((NB, 2, 4, 32, 768), BF),
            pltpu.VMEM((NB, 2, 3, 32, 768), BF),
            pltpu.VMEM((NB, 2, 4, 16, 384), BF),
            pltpu.VMEM((NB, 2, 3, 16, 384), BF),
            pltpu.VMEM((NB, 2, 4, 16, 384), BF),
            pltpu.VMEM((NB, 2, 4, 4, 16, 384), BF),
            pltpu.VMEM((NDP, CAP, PAIR), BF),
            pltpu.VMEM((NDP, CAP, PAIR), BF),
            pltpu.VMEM((rows, NDP * CAP), BF),
            pltpu.VMEM((rows, NDP * CAP), BF),
            pltpu.VMEM((rows, NDP * CAP), BF),
            dma((7,)),
            dma((6,)),
            dma((NZ,)),
            dma((NB,)),
            dma((NB,)),
            dma((NB,)),
            dma((NB,)),
            dma((1,)),
        ],
        compiler_params=pltpu.CompilerParams(
            collective_id=0, has_side_effects=True, vmem_limit_bytes=63 << 20
        ),
        cost_estimate=pl.CostEstimate(
            flops=6 * 2 * 512 * COLS * FF, bytes_accessed=4 << 20, transcendentals=1 << 16
        ),
    )(tokens.T, routes.T, route_weights.T, w_gate[0], w_up[0], w_down[0].T, cotangent.T)
    return mixed.T, grad.T


def solution(mesh):
    in_specs = (
        P("dp", "ctx"),
        P("dp", None),
        P("dp", None),
        P("dp", "ctx", None),
        P("dp", "ctx", None),
        P("dp", None, "ctx"),
        P("dp", "ctx"),
    )
    out_specs = (P("dp", "ctx"), P("dp", "ctx"))
    return jax.shard_map(shards, mesh=mesh, in_specs=in_specs, out_specs=out_specs, check_vma=False)
```

```python
import functools

import jax
import jax.numpy as jnp
from jax import lax
from jax.experimental import pallas as pl
from jax.experimental.pallas import tpu as pltpu
from jax.sharding import PartitionSpec as P

LOGICAL = pl.DeviceIdType.LOGICAL
BF = jnp.bfloat16
F32 = jnp.float32

NZ = 16
NDP = 32
CAP = 16
NB = 8
EARLY = 7
COLS = 448
PAIR = 2 * COLS
FF = 1024
PAD = 64


FAR = (2, 7, 6, 5, 4, 3, 1, 0)
PLAN = (
    (0, 0), (1, 0), (2, 0), (0, 1), (3, 0), (1, 1), (0, 2), (4, 0),
    (2, 1), (1, 2), (3, 1), (0, 3), (2, 2), (4, 1), (1, 3), (3, 2),
    (0, 4), (2, 3), (4, 2), (0, 5), (3, 3), (1, 4), (0, 6), (0, 7),
    (2, 4), (1, 5), (4, 3), (3, 4), (1, 6), (1, 7), (2, 5), (2, 6),
    (2, 7), (4, 4), (3, 5), (3, 6), (3, 7), (4, 5), (4, 6), (4, 7),
)


def entry(values, i):
    found = values[-1]
    for n, value in enumerate(values[:-1]):
        found = jnp.where(i == n, value, found)
    return found


def offset_at(b, g):
    far = entry(FAR, b)
    return far + 1 if g == 0 else -far


def wrap(i, n):
    return jnp.where(i < 0, i + n, jnp.where(i >= n, i - n, i))


def nt(a, b):
    return lax.dot_general(a, b, (((1,), (1,)), ((), ())), preferred_element_type=F32)


def nn(a, b):
    return jnp.dot(a, b, preferred_element_type=F32)


def kernel(
    tok_hbm, routes_hbm, rw_hbm, wg_hbm, wu_hbm, wd_hbm, cot_hbm,
    out_ref,
    tok, cot, routes, weights, wg, wu, wd,
    xs, xr, p1s, p1r, p2s, p2r, h1, h2, rs, rr, weigh_hi, weigh_lo, plain,
    in_sem, send_sem, x_sem, p1_sem, p2_sem, h1_sem, h2_sem, r_sem,
):
    dp = lax.axis_index("dp")
    ctx = lax.axis_index("ctx")
    z, core, y, x = dp // 2, dp % 2, ctx // 4, ctx % 4

    def await_bytes(ref, sem):
        pltpu.make_async_copy(ref, ref, sem).wait()

    barrier = pltpu.get_barrier_semaphore()

    def greet_dp(k, carry):
        pl.semaphore_signal(barrier, inc=1, device_id=wrap(dp + k, NDP) * 16 + ctx, device_id_type=LOGICAL)
        return carry

    def greet_ctx(k, carry):
        pl.semaphore_signal(barrier, inc=1, device_id=dp * 16 + wrap(ctx + k, 16), device_id_type=LOGICAL)
        return carry

    loads = [
        pltpu.make_async_copy(routes_hbm, routes, in_sem.at[5]),
        pltpu.make_async_copy(rw_hbm, weights, in_sem.at[6]),
        pltpu.make_async_copy(tok_hbm, tok, in_sem.at[0]),
        pltpu.make_async_copy(cot_hbm, cot, in_sem.at[1]),
        pltpu.make_async_copy(wg_hbm, wg.at[pl.ds(PAD, COLS)], in_sem.at[2]),
        pltpu.make_async_copy(wu_hbm, wu.at[pl.ds(PAD, COLS)], in_sem.at[3]),
        pltpu.make_async_copy(wd_hbm, wd.at[pl.ds(PAD, COLS)], in_sem.at[4]),
    ]
    for load in loads:
        load.start()
    lax.fori_loop(1, NDP, greet_dp, 0)
    lax.fori_loop(1, 16, greet_ctx, 0)

    loads[0].wait()
    loads[1].wait()
    r0, r1 = routes[0:1].astype(F32), routes[1:2].astype(F32)
    w0, w1 = weights[0:1], weights[1:2]
    rows = routes.shape[1]
    experts = lax.broadcasted_iota(jnp.int32, (NDP, rows), 0).astype(F32)
    oh0 = (r0 == experts).astype(F32)
    oh1 = (r1 == experts).astype(F32)
    earlier = (
        lax.broadcasted_iota(jnp.int32, (rows, rows), 0)
        < lax.broadcasted_iota(jnp.int32, (rows, rows), 1)
    ).astype(F32)
    before = nn((oh0 + oh1).astype(BF), earlier.astype(BF))
    s0 = jnp.sum(before * oh0, axis=0, keepdims=True)
    s1 = jnp.sum(before * oh1, axis=0, keepdims=True)
    c0, c1 = r0 * CAP + s0, r1 * CAP + s1
    places = lax.broadcasted_iota(jnp.int32, (NDP * CAP, rows), 0).astype(F32)
    hit0 = (c0 == places).astype(F32)
    hit1 = (c1 == places).astype(F32)
    loads[2].wait()
    loads[3].wait()
    tok_f, cot_f = tok[...].astype(F32), cot[...].astype(F32)
    both = jnp.concatenate(
        [
            jnp.concatenate([tok_f, tok_f], axis=1),
            jnp.concatenate([cot_f * w0, cot_f * w1], axis=1),
        ],
        axis=0,
    ).astype(BF)
    pick = jnp.concatenate([hit0, hit1], axis=1).astype(BF)
    xs[...] = nt(pick, both).astype(BF).reshape(NDP, CAP, PAIR)

    pl.semaphore_wait(barrier, NDP - 1 + 15)

    def z_send(src, dst, dst_dp, kind, recv):
        pltpu.make_async_remote_copy(
            src_ref=src, dst_ref=dst, send_sem=send_sem.at[kind], recv_sem=recv,
            device_id=dst_dp * 16 + ctx, device_id_type=LOGICAL,
        ).start()

    def dispatch(b, carry):
        for g in range(2):
            off = offset_at(b, g)
            for c in range(2):
                dst = wrap(z - off, NZ) * 2 + c

                @pl.when(dst != dp)
                def _():
                    z_send(xs.at[dst], xr.at[dp], dst, 0, x_sem.at[2 * b + g])

        return carry

    lax.fori_loop(0, NB, dispatch, 0)
    xr[dp] = xs[dp]

    zero = jnp.zeros((PAD, FF), BF)
    for w in (wg, wu, wd):
        w[0:PAD] = zero
        w[PAD + COLS :] = zero
    pair_places = lax.broadcasted_iota(jnp.int32, (2 * CAP, rows), 0)
    places = jnp.concatenate(
        [
            (pair_places + wrap(z - off, NZ) * 2 * CAP).astype(F32)
            for far in FAR
            for off in (far + 1, -far)
        ],
        axis=0,
    )
    hit0 = (c0 == places).astype(F32)
    hit1 = (c1 == places).astype(F32)
    weighted = (hit0 * w0 + hit1 * w1).T
    high = weighted.astype(BF)
    weigh_hi[...] = high
    weigh_lo[...] = (weighted - high.astype(F32)).astype(BF)
    plain[...] = (hit0 + hit1).T.astype(BF)
    for load in loads[4:]:
        load.wait()

    x_at = [wrap(x + d, 4) for d in range(4)]
    y_at = [wrap(y + d, 4) for d in range(4)]
    peers = {
        True: [dp * 16 + y * 4 + x_at[d] for d in range(1, 4)],
        False: [dp * 16 + y_at[d] * 4 + x for d in range(1, 4)],
    }

    def send(src, dst, kind, recv, along_x, d):
        pltpu.make_async_remote_copy(
            src_ref=src, dst_ref=dst, send_sem=send_sem.at[kind], recv_sem=recv,
            device_id=peers[along_x][d - 1], device_id_type=LOGICAL,
        ).start()

    def first(g, d=0):
        return x_at[d] if g == 0 else y_at[d]

    def second(g, d=0):
        return y_at[d] if g == 0 else x_at[d]

    def products(b):
        await_bytes(xr.at[pl.ds(0, 2)], x_sem.at[2 * b])

        here = offset_at(b, 1) == 0

        @pl.when(here)
        def _():
            await_bytes(xr.at[pl.ds(0, 1)], x_sem.at[2 * b + 1])

        @pl.when(jnp.logical_not(here))
        def _():
            await_bytes(xr.at[pl.ds(0, 2)], x_sem.at[2 * b + 1])

        block = jnp.concatenate(
            [
                xr[pl.ds(2 * wrap(z + offset_at(b, g), NZ), 2)].reshape(2 * CAP, PAIR)
                for g in range(2)
            ],
            axis=0,
        )
        left, right = block[:, 0:512], block[:, 384:896]
        parts = (
            nn(left, wg[PAD : PAD + 512]),
            nn(left, wu[PAD : PAD + 512]),
            nn(right, wd[0:512]),
        )
        for g in range(2):
            for p in range(4):
                for a in range(3):
                    p1s[b, g, p, :, a * 256 : a * 256 + 256] = parts[a][
                        g * 32 : g * 32 + 32, p * 256 : p * 256 + 256
                    ].astype(BF)
        for d in range(1, 4):
            for g in range(2):
                send(
                    p1s.at[b, g, first(g, d)], p1r.at[b, g, d - 1], 1, p1_sem.at[b], g == 0, d
                )

    def add_first(b):
        await_bytes(p1r.at[b], p1_sem.at[b])
        for g in range(2):
            total = p1s[b, g, first(g)].astype(F32)
            for d in range(3):
                total = total + p1r[b, g, d].astype(F32)
            for q in range(4):
                for a in range(3):
                    lane = a * 256 + 128 * (q % 2)
                    p2s[b, g, q, :, a * 128 : a * 128 + 128] = total[
                        16 * (q // 2) : 16 * (q // 2) + 16, lane : lane + 128
                    ].astype(BF)
        for d in range(1, 4):
            for g in range(2):
                send(
                    p2s.at[b, g, second(g, d)], p2r.at[b, g, d - 1], 2, p2_sem.at[b], g == 1, d
                )

    def add_second(b):
        await_bytes(p2r.at[b], p2_sem.at[b])
        for g in range(2):
            total = p2s[b, g, second(g)].astype(F32)
            for d in range(3):
                total = total + p2r[b, g, d].astype(F32)
            gate, up, hidden_grad = total[:, 0:128], total[:, 128:256], total[:, 256:384]
            sig = jax.nn.sigmoid(gate)
            h1[b, g, second(g), :, 0:128] = (gate * sig * up).astype(BF)
            h1[b, g, second(g), :, 128:256] = (
                hidden_grad * up * sig * (1.0 + gate * (1.0 - sig))
            ).astype(BF)
            h1[b, g, second(g), :, 256:384] = (hidden_grad * gate * sig).astype(BF)
        for d in range(1, 4):
            for g in range(2):
                mine = h1.at[b, g, second(g)]
                send(mine, mine, 3, h1_sem.at[b], g == 1, d)

    def spread(b):
        await_bytes(p2r.at[b], h1_sem.at[b])
        for d in range(1, 4):
            for g in range(2):
                send(h1.at[b, g], h2.at[b, g, first(g)], 4, h2_sem.at[b], g == 0, d)
        for g in range(2):
            h2[b, g, first(g)] = h1[b, g]

    def give_back(b):
        await_bytes(p1r.at[b], h2_sem.at[b])

        def whole(a):
            return jnp.concatenate(
                [
                    jnp.concatenate(
                        [
                            h2[b, g, p, 2 * half + q, :, a * 128 : a * 128 + 128]
                            for p in range(4)
                            for q in range(2)
                        ],
                        axis=1,
                    )
                    for g in range(2)
                    for half in range(2)
                ],
                axis=0,
            )

        out = nt(whole(0), wd[PAD : PAD + 512])
        row_grad = nt(whole(1), wg[0:512]) + nt(whole(2), wu[0:512])
        pair = jnp.concatenate(
            [out[:, 0:384], out[:, 384:512] + row_grad[:, 0:128], row_grad[:, 128:512]], axis=1
        ).astype(BF)
        late = jnp.where(b < EARLY, 0, 1)
        for g in range(2):
            off = offset_at(b, g)
            back = 2 * (2 * b + g) + core
            for c in range(2):
                dst = wrap(z + off, NZ) * 2 + c
                at = (2 * g + c) * CAP
                rs[dst] = pair[at : at + CAP]

                @pl.when(dst != dp)
                def _():
                    z_send(rs.at[dst], rr.at[back], dst, 5, r_sem.at[late])

    stages = (products, add_first, add_second, spread, give_back)

    def step(n, carry):
        code = entry(tuple(s * NB + b for s, b in PLAN), n)
        for s, work in enumerate(stages):

            @pl.when((code >= s * NB) & (code < s * NB + NB))
            def _():
                work(code - s * NB)

        return carry

    lax.fori_loop(0, len(PLAN), step, 0)
    rr[2 * (2 * FAR.index(0) + 1) + core] = rs[dp]

    def summed(first, last):
        back = rr[4 * first : 4 * last].reshape((last - first) * 4 * CAP, PAIR)
        part = pl.ds(first * 4 * CAP, (last - first) * 4 * CAP)
        mixed = nn(weigh_hi[:, part], back[:, 0:512]) + nn(weigh_lo[:, part], back[:, 0:512])
        return mixed, nn(plain[:, part], back[:, 384:896])

    await_bytes(rr.at[pl.ds(0, 4 * EARLY)], r_sem.at[0])
    mixed, grad = summed(0, EARLY)
    await_bytes(rr.at[pl.ds(0, 4 * (NB - EARLY) - 1)], r_sem.at[1])
    mixed_late, grad_late = summed(EARLY, NB)
    out_ref[0] = (mixed + mixed_late).T[0:COLS].astype(BF)
    out_ref[1] = (grad + grad_late).T[PAD:].astype(BF)

    await_bytes(xs.at[pl.ds(0, NDP - 1)], send_sem.at[0])
    await_bytes(p1r, send_sem.at[1])
    await_bytes(p2r, send_sem.at[2])
    await_bytes(p2r, send_sem.at[3])
    await_bytes(p1r, send_sem.at[4])
    await_bytes(xs.at[pl.ds(0, NDP - 1)], send_sem.at[5])


def shards(tokens, routes, route_weights, w_gate, w_up, w_down, cotangent):
    rows, cols = tokens.shape
    hbm = pl.BlockSpec(memory_space=pltpu.HBM)
    vmem = pl.BlockSpec(memory_space=pltpu.VMEM)
    dma = pltpu.SemaphoreType.DMA
    out = jax.ShapeDtypeStruct((2, cols, rows), BF)
    both = pl.pallas_call(
        kernel,
        out_shape=out,
        in_specs=[hbm, hbm, hbm, hbm, hbm, hbm, hbm],
        out_specs=vmem,
        scratch_shapes=[
            pltpu.VMEM((cols, rows), BF),
            pltpu.VMEM((cols, rows), BF),
            pltpu.VMEM(routes.shape[::-1], jnp.int32),
            pltpu.VMEM(routes.shape[::-1], F32),
            pltpu.VMEM((PAD + COLS + PAD, FF), BF),
            pltpu.VMEM((PAD + COLS + PAD, FF), BF),
            pltpu.VMEM((PAD + COLS + PAD, FF), BF),
            pltpu.VMEM((NDP, CAP, PAIR), BF),
            pltpu.VMEM((NDP, CAP, PAIR), BF),
            pltpu.VMEM((NB, 2, 4, 32, 768), BF),
            pltpu.VMEM((NB, 2, 3, 32, 768), BF),
            pltpu.VMEM((NB, 2, 4, 16, 384), BF),
            pltpu.VMEM((NB, 2, 3, 16, 384), BF),
            pltpu.VMEM((NB, 2, 4, 16, 384), BF),
            pltpu.VMEM((NB, 2, 4, 4, 16, 384), BF),
            pltpu.VMEM((NDP, CAP, PAIR), BF),
            pltpu.VMEM((NDP, CAP, PAIR), BF),
            pltpu.VMEM((rows, NDP * CAP), BF),
            pltpu.VMEM((rows, NDP * CAP), BF),
            pltpu.VMEM((rows, NDP * CAP), BF),
            dma((7,)),
            dma((6,)),
            dma((NZ,)),
            dma((NB,)),
            dma((NB,)),
            dma((NB,)),
            dma((NB,)),
            dma((2,)),
        ],
        compiler_params=pltpu.CompilerParams(
            collective_id=0, has_side_effects=True, vmem_limit_bytes=63 << 20
        ),
        cost_estimate=pl.CostEstimate(
            flops=6 * 2 * 512 * COLS * FF, bytes_accessed=4 << 20, transcendentals=1 << 16
        ),
    )(tokens.T, routes.T, route_weights.T, w_gate[0], w_up[0], w_down[0].T, cotangent.T)
    return both[0].T, both[1].T


def solution(mesh):
    in_specs = (
        P("dp", "ctx"),
        P("dp", None),
        P("dp", None),
        P("dp", "ctx", None),
        P("dp", "ctx", None),
        P("dp", None, "ctx"),
        P("dp", "ctx"),
    )
    out_specs = (P("dp", "ctx"), P("dp", "ctx"))
    return jax.shard_map(shards, mesh=mesh, in_specs=in_specs, out_specs=out_specs, check_vma=False)
```

```python
import functools

import jax
import jax.numpy as jnp
from jax import lax
from jax.experimental import pallas as pl
from jax.experimental.pallas import tpu as pltpu
from jax.sharding import PartitionSpec as P

LOGICAL = pl.DeviceIdType.LOGICAL
BF = jnp.bfloat16
F32 = jnp.float32

NZ = 16
NDP = 32
CAP = 16
NB = 8
EARLY = 7
COLS = 448
PAIR = 2 * COLS
FF = 1024
PAD = 64


FAR = (2, 7, 6, 5, 4, 3, 1, 0)
PLAN = (
    (0, 0), (1, 0), (2, 0), (0, 1), (3, 0), (1, 1), (0, 2), (4, 0),
    (2, 1), (1, 2), (3, 1), (0, 3), (2, 2), (4, 1), (1, 3), (3, 2),
    (0, 4), (2, 3), (4, 2), (0, 5), (3, 3), (1, 4), (0, 6), (0, 7),
    (2, 4), (1, 5), (4, 3), (3, 4), (1, 6), (1, 7), (2, 5), (2, 6),
    (2, 7), (4, 4), (3, 5), (3, 6), (3, 7), (4, 5), (4, 6), (4, 7),
)


def entry(values, i):
    if isinstance(i, int):
        return values[i]
    found = values[-1]
    for n, value in enumerate(values[:-1]):
        found = jnp.where(i == n, value, found)
    return found


def offset_at(b, g):
    far = entry(FAR, b)
    return far + 1 if g == 0 else -far


def wrap(i, n):
    return jnp.where(i < 0, i + n, jnp.where(i >= n, i - n, i))


def nt(a, b):
    return lax.dot_general(a, b, (((1,), (1,)), ((), ())), preferred_element_type=F32)


def nn(a, b):
    return jnp.dot(a, b, preferred_element_type=F32)


def kernel(
    tok_hbm, routes_hbm, rw_hbm, wg_hbm, wu_hbm, wd_hbm, cot_hbm,
    out_ref,
    tok, cot, routes, weights, wg, wu, wd,
    xs, xr, p1s, p1r, p2s, p2r, h1, h2, rs, rr, weigh_hi, weigh_lo, plain,
    in_sem, send_sem, x_sem, p1_sem, p2_sem, h1_sem, h2_sem, r_sem,
):
    dp = lax.axis_index("dp")
    ctx = lax.axis_index("ctx")
    z, core, y, x = dp // 2, dp % 2, ctx // 4, ctx % 4

    def await_bytes(ref, sem):
        pltpu.make_async_copy(ref, ref, sem).wait()

    barrier = pltpu.get_barrier_semaphore()

    def greet_dp(k, carry):
        pl.semaphore_signal(barrier, inc=1, device_id=wrap(dp + k, NDP) * 16 + ctx, device_id_type=LOGICAL)
        return carry

    def greet_ctx(k, carry):
        pl.semaphore_signal(barrier, inc=1, device_id=dp * 16 + wrap(ctx + k, 16), device_id_type=LOGICAL)
        return carry

    loads = [
        pltpu.make_async_copy(routes_hbm, routes, in_sem.at[5]),
        pltpu.make_async_copy(rw_hbm, weights, in_sem.at[6]),
        pltpu.make_async_copy(tok_hbm, tok, in_sem.at[0]),
        pltpu.make_async_copy(cot_hbm, cot, in_sem.at[1]),
        pltpu.make_async_copy(wg_hbm, wg.at[pl.ds(PAD, COLS)], in_sem.at[2]),
        pltpu.make_async_copy(wu_hbm, wu.at[pl.ds(PAD, COLS)], in_sem.at[3]),
        pltpu.make_async_copy(wd_hbm, wd.at[pl.ds(PAD, COLS)], in_sem.at[4]),
    ]
    for load in loads:
        load.start()
    lax.fori_loop(1, NDP, greet_dp, 0)
    lax.fori_loop(1, 16, greet_ctx, 0)

    loads[0].wait()
    loads[1].wait()
    r0, r1 = routes[0:1].astype(F32), routes[1:2].astype(F32)
    w0, w1 = weights[0:1], weights[1:2]
    rows = routes.shape[1]
    experts = lax.broadcasted_iota(jnp.int32, (NDP, rows), 0).astype(F32)
    oh0 = (r0 == experts).astype(F32)
    oh1 = (r1 == experts).astype(F32)
    earlier = (
        lax.broadcasted_iota(jnp.int32, (rows, rows), 0)
        < lax.broadcasted_iota(jnp.int32, (rows, rows), 1)
    ).astype(F32)
    before = nn((oh0 + oh1).astype(BF), earlier.astype(BF))
    s0 = jnp.sum(before * oh0, axis=0, keepdims=True)
    s1 = jnp.sum(before * oh1, axis=0, keepdims=True)
    c0, c1 = r0 * CAP + s0, r1 * CAP + s1
    places = lax.broadcasted_iota(jnp.int32, (NDP * CAP, rows), 0).astype(F32)
    hit0 = (c0 == places).astype(F32)
    hit1 = (c1 == places).astype(F32)
    loads[2].wait()
    loads[3].wait()
    tok_f, cot_f = tok[...].astype(F32), cot[...].astype(F32)
    both = jnp.concatenate(
        [
            jnp.concatenate([tok_f, tok_f], axis=1),
            jnp.concatenate([cot_f * w0, cot_f * w1], axis=1),
        ],
        axis=0,
    ).astype(BF)
    pick = jnp.concatenate([hit0, hit1], axis=1).astype(BF)
    xs[...] = nt(pick, both).astype(BF).reshape(NDP, CAP, PAIR)

    pl.semaphore_wait(barrier, NDP - 1 + 15)

    def z_send(src, dst, dst_dp, kind, recv):
        pltpu.make_async_remote_copy(
            src_ref=src, dst_ref=dst, send_sem=send_sem.at[kind], recv_sem=recv,
            device_id=dst_dp * 16 + ctx, device_id_type=LOGICAL,
        ).start()

    def dispatch(b, carry):
        for g in range(2):
            off = offset_at(b, g)
            for c in range(2):
                dst = wrap(z - off, NZ) * 2 + c

                @pl.when(dst != dp)
                def _():
                    z_send(xs.at[dst], xr.at[dp], dst, 0, x_sem.at[2 * b + g])

        return carry

    lax.fori_loop(0, NB, dispatch, 0)
    xr[dp] = xs[dp]

    zero = jnp.zeros((PAD, FF), BF)
    for w in (wg, wu, wd):
        w[0:PAD] = zero
        w[PAD + COLS :] = zero
    pair_places = lax.broadcasted_iota(jnp.int32, (2 * CAP, rows), 0)
    places = jnp.concatenate(
        [
            (pair_places + wrap(z - off, NZ) * 2 * CAP).astype(F32)
            for far in FAR
            for off in (far + 1, -far)
        ],
        axis=0,
    )
    hit0 = (c0 == places).astype(F32)
    hit1 = (c1 == places).astype(F32)
    weighted = (hit0 * w0 + hit1 * w1).T
    high = weighted.astype(BF)
    weigh_hi[...] = high
    weigh_lo[...] = (weighted - high.astype(F32)).astype(BF)
    plain[...] = (hit0 + hit1).T.astype(BF)
    for load in loads[4:]:
        load.wait()

    x_at = [wrap(x + d, 4) for d in range(4)]
    y_at = [wrap(y + d, 4) for d in range(4)]
    peers = {
        True: [dp * 16 + y * 4 + x_at[d] for d in range(1, 4)],
        False: [dp * 16 + y_at[d] * 4 + x for d in range(1, 4)],
    }

    def send(src, dst, kind, recv, along_x, d):
        pltpu.make_async_remote_copy(
            src_ref=src, dst_ref=dst, send_sem=send_sem.at[kind], recv_sem=recv,
            device_id=peers[along_x][d - 1], device_id_type=LOGICAL,
        ).start()

    def first(g, d=0):
        return x_at[d] if g == 0 else y_at[d]

    def second(g, d=0):
        return y_at[d] if g == 0 else x_at[d]

    def products(b):
        await_bytes(xr.at[pl.ds(0, 2)], x_sem.at[2 * b])

        here = jnp.asarray(offset_at(b, 1) == 0)

        @pl.when(here)
        def _():
            await_bytes(xr.at[pl.ds(0, 1)], x_sem.at[2 * b + 1])

        @pl.when(jnp.logical_not(here))
        def _():
            await_bytes(xr.at[pl.ds(0, 2)], x_sem.at[2 * b + 1])

        block = jnp.concatenate(
            [
                xr[pl.ds(2 * wrap(z + offset_at(b, g), NZ), 2)].reshape(2 * CAP, PAIR)
                for g in range(2)
            ],
            axis=0,
        )
        left, right = block[:, 0:512], block[:, 384:896]
        parts = (
            nn(left, wg[PAD : PAD + 512]),
            nn(left, wu[PAD : PAD + 512]),
            nn(right, wd[0:512]),
        )
        for g in range(2):
            for p in range(4):
                for a in range(3):
                    p1s[b, g, p, :, a * 256 : a * 256 + 256] = parts[a][
                        g * 32 : g * 32 + 32, p * 256 : p * 256 + 256
                    ].astype(BF)
        for d in range(1, 4):
            for g in range(2):
                send(
                    p1s.at[b, g, first(g, d)], p1r.at[b, g, d - 1], 1, p1_sem.at[b], g == 0, d
                )

    def add_first(b):
        await_bytes(p1r.at[b], p1_sem.at[b])
        for g in range(2):
            total = p1s[b, g, first(g)].astype(F32)
            for d in range(3):
                total = total + p1r[b, g, d].astype(F32)
            for q in range(4):
                for a in range(3):
                    lane = a * 256 + 128 * (q % 2)
                    p2s[b, g, q, :, a * 128 : a * 128 + 128] = total[
                        16 * (q // 2) : 16 * (q // 2) + 16, lane : lane + 128
                    ].astype(BF)
        for d in range(1, 4):
            for g in range(2):
                send(
                    p2s.at[b, g, second(g, d)], p2r.at[b, g, d - 1], 2, p2_sem.at[b], g == 1, d
                )

    def add_second(b):
        await_bytes(p2r.at[b], p2_sem.at[b])
        for g in range(2):
            total = p2s[b, g, second(g)].astype(F32)
            for d in range(3):
                total = total + p2r[b, g, d].astype(F32)
            gate, up, hidden_grad = total[:, 0:128], total[:, 128:256], total[:, 256:384]
            sig = jax.nn.sigmoid(gate)
            h1[b, g, second(g), :, 0:128] = (gate * sig * up).astype(BF)
            h1[b, g, second(g), :, 128:256] = (
                hidden_grad * up * sig * (1.0 + gate * (1.0 - sig))
            ).astype(BF)
            h1[b, g, second(g), :, 256:384] = (hidden_grad * gate * sig).astype(BF)
        for d in range(1, 4):
            for g in range(2):
                mine = h1.at[b, g, second(g)]
                send(mine, mine, 3, h1_sem.at[b], g == 1, d)

    def spread(b):
        await_bytes(p2r.at[b], h1_sem.at[b])
        for d in range(1, 4):
            for g in range(2):
                send(h1.at[b, g], h2.at[b, g, first(g)], 4, h2_sem.at[b], g == 0, d)
        for g in range(2):
            h2[b, g, first(g)] = h1[b, g]

    def give_back(b):
        await_bytes(p1r.at[b], h2_sem.at[b])

        def whole(a):
            return jnp.concatenate(
                [
                    jnp.concatenate(
                        [
                            h2[b, g, p, 2 * half + q, :, a * 128 : a * 128 + 128]
                            for p in range(4)
                            for q in range(2)
                        ],
                        axis=1,
                    )
                    for g in range(2)
                    for half in range(2)
                ],
                axis=0,
            )

        out = nt(whole(0), wd[PAD : PAD + 512])
        row_grad = nt(whole(1), wg[0:512]) + nt(whole(2), wu[0:512])
        pair = jnp.concatenate(
            [out[:, 0:384], out[:, 384:512] + row_grad[:, 0:128], row_grad[:, 128:512]], axis=1
        ).astype(BF)
        late = jnp.where(b < EARLY, 0, 1)
        for g in range(2):
            off = offset_at(b, g)
            back = 2 * (2 * b + g) + core
            for c in range(2):
                dst = wrap(z + off, NZ) * 2 + c
                at = (2 * g + c) * CAP
                rs[dst] = pair[at : at + CAP]

                @pl.when(dst != dp)
                def _():
                    z_send(rs.at[dst], rr.at[back], dst, 5, r_sem.at[late])

    stages = (products, add_first, add_second, spread, give_back)

    for s, b in PLAN:
        stages[s](b)
    rr[2 * (2 * FAR.index(0) + 1) + core] = rs[dp]

    def summed(first, last):
        back = rr[4 * first : 4 * last].reshape((last - first) * 4 * CAP, PAIR)
        part = pl.ds(first * 4 * CAP, (last - first) * 4 * CAP)
        mixed = nn(weigh_hi[:, part], back[:, 0:512]) + nn(weigh_lo[:, part], back[:, 0:512])
        return mixed, nn(plain[:, part], back[:, 384:896])

    await_bytes(rr.at[pl.ds(0, 4 * EARLY)], r_sem.at[0])
    mixed, grad = summed(0, EARLY)
    await_bytes(rr.at[pl.ds(0, 4 * (NB - EARLY) - 1)], r_sem.at[1])
    mixed_late, grad_late = summed(EARLY, NB)
    out_ref[0] = (mixed + mixed_late).T[0:COLS].astype(BF)
    out_ref[1] = (grad + grad_late).T[PAD:].astype(BF)

    await_bytes(xs.at[pl.ds(0, NDP - 1)], send_sem.at[0])
    await_bytes(p1r, send_sem.at[1])
    await_bytes(p2r, send_sem.at[2])
    await_bytes(p2r, send_sem.at[3])
    await_bytes(p1r, send_sem.at[4])
    await_bytes(xs.at[pl.ds(0, NDP - 1)], send_sem.at[5])


def shards(tokens, routes, route_weights, w_gate, w_up, w_down, cotangent):
    rows, cols = tokens.shape
    hbm = pl.BlockSpec(memory_space=pltpu.HBM)
    vmem = pl.BlockSpec(memory_space=pltpu.VMEM)
    dma = pltpu.SemaphoreType.DMA
    out = jax.ShapeDtypeStruct((2, cols, rows), BF)
    both = pl.pallas_call(
        kernel,
        out_shape=out,
        in_specs=[hbm, hbm, hbm, hbm, hbm, hbm, hbm],
        out_specs=vmem,
        scratch_shapes=[
            pltpu.VMEM((cols, rows), BF),
            pltpu.VMEM((cols, rows), BF),
            pltpu.VMEM(routes.shape[::-1], jnp.int32),
            pltpu.VMEM(routes.shape[::-1], F32),
            pltpu.VMEM((PAD + COLS + PAD, FF), BF),
            pltpu.VMEM((PAD + COLS + PAD, FF), BF),
            pltpu.VMEM((PAD + COLS + PAD, FF), BF),
            pltpu.VMEM((NDP, CAP, PAIR), BF),
            pltpu.VMEM((NDP, CAP, PAIR), BF),
            pltpu.VMEM((NB, 2, 4, 32, 768), BF),
            pltpu.VMEM((NB, 2, 3, 32, 768), BF),
            pltpu.VMEM((NB, 2, 4, 16, 384), BF),
            pltpu.VMEM((NB, 2, 3, 16, 384), BF),
            pltpu.VMEM((NB, 2, 4, 16, 384), BF),
            pltpu.VMEM((NB, 2, 4, 4, 16, 384), BF),
            pltpu.VMEM((NDP, CAP, PAIR), BF),
            pltpu.VMEM((NDP, CAP, PAIR), BF),
            pltpu.VMEM((rows, NDP * CAP), BF),
            pltpu.VMEM((rows, NDP * CAP), BF),
            pltpu.VMEM((rows, NDP * CAP), BF),
            dma((7,)),
            dma((6,)),
            dma((NZ,)),
            dma((NB,)),
            dma((NB,)),
            dma((NB,)),
            dma((NB,)),
            dma((2,)),
        ],
        compiler_params=pltpu.CompilerParams(
            collective_id=0, has_side_effects=True, vmem_limit_bytes=63 << 20
        ),
        cost_estimate=pl.CostEstimate(
            flops=6 * 2 * 512 * COLS * FF, bytes_accessed=4 << 20, transcendentals=1 << 16
        ),
    )(tokens.T, routes.T, route_weights.T, w_gate[0], w_up[0], w_down[0].T, cotangent.T)
    return both[0].T, both[1].T


def solution(mesh):
    in_specs = (
        P("dp", "ctx"),
        P("dp", None),
        P("dp", None),
        P("dp", "ctx", None),
        P("dp", "ctx", None),
        P("dp", None, "ctx"),
        P("dp", "ctx"),
    )
    out_specs = (P("dp", "ctx"), P("dp", "ctx"))
    return jax.shard_map(shards, mesh=mesh, in_specs=in_specs, out_specs=out_specs, check_vma=False)
```
